32 devices in a mesh: groups: 2 (over y), patch: 4 (over z), fsdp: 2 (over x), cfg: 2 (over core).
Axes of the slice: x: 2, y: 2, z: 4, core: 2. Of those that a mesh axis runs over, the one named last changes fastest.
Arguments:
- hidden_states: bfloat16 [4, 1536, 5120], P(('groups', 'cfg'), 'patch', 'fsdp'), parts along dimension 0, may hold values from -6 to 6
- queries: bfloat16 [4, 1536, 2560], P(('groups', 'cfg'), 'patch', 'fsdp'), parts along dimension 0, may hold values from -8 to 8
- fresh_kv: bfloat16 [4, 2, 1536, 2560], P(('groups', 'cfg'), None, 'patch', 'fsdp'), parts along dimension 0, may hold values from -8 to 8
- stale_kv: bfloat16 [4, 2, 1536, 2560], P(('groups', 'cfg'), None, 'patch', 'fsdp'), parts along dimension 0, may hold values from -8 to 8
- out_weight: bfloat16 [2560, 5120], P('fsdp'), may hold values from -0.125 to 0.125
- gate_table: float32 [50, 5120], P(None, 'fsdp'), may hold values from -4 to 4
- timestep: int32 [2], P('groups'), parts along dimension 0, may hold values from 0 to 49
Outputs:
- block_out: bfloat16 [4, 1536, 5120], P(('groups', 'cfg'), 'patch', 'fsdp'), parts along dimension 0
The draws below stay inside these ranges and needn't reach their ends.
There are 2 independent parts, one for each index of `groups`. The reference program is written for one: setup_inputs(seed, part) draws one part's arguments, and reference() takes and returns one part's arrays. A program takes and returns all parts, laid end to end along the dimension named above; an argument that names none is the same for every part. Nothing has to cross between parts.
All inputs are finite; a program needn't handle non-finite values.
Results may differ from the reference program's by a relative error of at most 0.0065.
Values may be sent and summed in bfloat16 or wider, within the bound.
A program may use at most 128 MiB of HBM per device.

```python
import jax
import jax.numpy as jnp
from jax import lax

D = 5120
HEADS = 20
HEAD = 128
STEPS = 50
TOK_DEV = 384
TOKENS = 1536
HD = 2560
N_PATCH = 4
N_FSDP = 2


def draw_queries(key, part):
    key = jax.random.fold_in(key, 11)
    base = jax.random.normal(key, (2, TOKENS, HEADS * HEAD), jnp.float32)
    values = jnp.clip(base * 1.6, -8.0, 8.0)
    return values.astype(jnp.bfloat16)


def draw_fresh_kv(key, part):
    key = jax.random.fold_in(key, 12)
    spread = jnp.array([1.6, 1.0], jnp.float32)[None, :, None, None]
    base = jax.random.normal(key, (2, 2, TOKENS, HEADS * HEAD), jnp.float32)
    values = jnp.clip(base * spread, -8.0, 8.0)
    return values.astype(jnp.bfloat16)


def draw_stale_kv(key, part):
    key = jax.random.fold_in(key, 13)
    spread = jnp.array([1.6, 1.0], jnp.float32)[None, :, None, None]
    base = jax.random.normal(key, (2, 2, TOKENS, HEADS * HEAD), jnp.float32)
    values = jnp.clip(base * spread, -8.0, 8.0)
    return values.astype(jnp.bfloat16)


def shard_levels(rng, dims, split, low, high):
    def one(axis_at, parts):
        steps = jax.random.uniform(jax.random.fold_in(jax.random.fold_in(rng, 6), axis_at), (parts,), jnp.float32, low / len(split), high / len(split))
        return jnp.repeat(jnp.exp(steps), dims[axis_at] // parts).reshape((-1,) + (1,) * (len(dims) - axis_at - 1))

    loudness = one(*split[0])
    for cut in split[1:]:
        loudness = loudness * one(*cut)
    return loudness


def noise(own_key, extent, scale, limit, split=(), held_as=jnp.bfloat16):
    values = scale * jax.random.normal(own_key, extent, jnp.float32)
    if split:
        values = values * shard_levels(own_key, extent, split, -0.22, 0.18)
    return jnp.clip(values, -limit, limit).astype(held_as)


def setup_inputs(seed: int = 0, part: int = 0) -> dict:
    streams_of = jax.random.split(jax.random.key(seed), 8)
    part_keys = jax.random.split(jax.random.fold_in(streams_of[7], part), 8)
    return {
        "hidden_states": noise(part_keys[0], (2, TOKENS, D), 1.0, 6.0, ((0, 2), (1, 4), (2, 2))),
        "queries": draw_queries(jax.random.fold_in(jax.random.fold_in(streams_of[7], part), 71), part),
        "fresh_kv": draw_fresh_kv(jax.random.fold_in(jax.random.fold_in(streams_of[7], part), 71), part),
        "stale_kv": draw_stale_kv(jax.random.fold_in(jax.random.fold_in(streams_of[7], part), 71), part),
        "out_weight": noise(streams_of[4], (HD, D), HD ** -0.5, 0.125, ((0, 2),)),
        "gate_table": noise(streams_of[5], (STEPS, D), 1.0, 4.0, ((1, 2),), jnp.float32),
        "timestep": jax.random.randint(part_keys[6], (1,), 0, STEPS).astype(jnp.int32),
    }


def attend(query_rows, key_rows, value_rows):
    score_scale = HEAD ** -0.5
    query_heads = query_rows.astype(jnp.float32).reshape(TOK_DEV, HEADS, HEAD)
    key_heads = key_rows.astype(jnp.float32).reshape(TOKENS, HEADS, HEAD)
    value_heads = value_rows.astype(jnp.float32).reshape(TOKENS, HEADS, HEAD)
    scores = jnp.einsum("qhd,khd->hqk", query_heads, key_heads) * score_scale
    peak = jnp.max(scores, axis=-1, keepdims=True)
    weights = jnp.exp(scores - peak)
    total = jnp.sum(weights, axis=-1, keepdims=True)
    probs = lax.optimization_barrier(weights.astype(jnp.bfloat16)).astype(jnp.float32)
    summed = jnp.einsum("hqk,khd->hqd", probs, value_heads) / total
    return jnp.transpose(summed, (1, 0, 2)).reshape(TOK_DEV, HEADS * HEAD).astype(jnp.bfloat16)


def reference(hidden_states, queries, fresh_kv, stale_kv, out_weight, gate_table, timestep):
    gate_row = lax.dynamic_index_in_dim(gate_table, timestep[0], 0, keepdims=False)
    block_width = HEADS * HEAD // N_FSDP
    results = []
    for branch in range(2):
        def one_patch(index):
            start = (index * TOK_DEV).astype(jnp.int32)
            query_rows = lax.dynamic_slice_in_dim(queries[branch], start, TOK_DEV, 0)
            own_rows = lax.dynamic_slice_in_dim(fresh_kv[branch], start, TOK_DEV, 1)
            seen = lax.dynamic_update_slice_in_dim(stale_kv[branch], own_rows, start, 1)
            return attend(query_rows, seen[0], seen[1])

        attention = lax.map(one_patch, jnp.arange(N_PATCH, dtype=jnp.int32)).reshape(TOKENS, HEADS * HEAD)
        projected = jnp.zeros((TOKENS, D), jnp.float32)
        for block in range(N_FSDP):
            lo = block * block_width
            term = jnp.dot(attention[:, lo:lo + block_width], out_weight[lo:lo + block_width, :], preferred_element_type=jnp.float32)
            projected = projected + lax.optimization_barrier(term.astype(jnp.bfloat16)).astype(jnp.float32)
        branch_out = hidden_states[branch].astype(jnp.float32) + gate_row[None, :] * projected
        results.append(branch_out.astype(jnp.bfloat16))
    return jnp.stack(results, axis=0)
```

```python
import functools
import math

import jax
import jax.numpy as jnp
from jax import lax
from jax.experimental import pallas as pl
from jax.experimental.pallas import tpu as pltpu
from jax.sharding import PartitionSpec as P

HEAD = 128


def dense_head(query_head, key_head, value_head):
    scores = jnp.einsum(
        "qd,kd->qk", query_head, key_head, preferred_element_type=jnp.float32
    ) * HEAD ** (-0.5)
    peak = jnp.max(scores, axis=-1, keepdims=True)
    weights = jnp.exp(scores - peak)
    total = jnp.sum(weights, axis=-1, keepdims=True)
    probs = weights.astype(jnp.bfloat16)
    return jnp.dot(probs, value_head, preferred_element_type=jnp.float32) / total


def local(hidden_states, queries, fresh_kv, stale_kv, out_weight, gate_table, timestep):
    rows_here = queries.shape[1]
    width = queries.shape[2]
    heads_here = width // HEAD
    query_local = queries[0]
    own_start = lax.axis_index("patch") * rows_here
    head_ids = jnp.arange(heads_here, dtype=jnp.int32)
    gathered = lax.all_gather(stale_kv, "patch", axis=2, tiled=True)[0]
    merged = lax.dynamic_update_slice_in_dim(gathered, fresh_kv[0], own_start, 1)

    def one_head(head):
        offset = head * HEAD
        query_head = lax.dynamic_slice_in_dim(query_local, offset, HEAD, 1)
        key_head = lax.dynamic_slice_in_dim(merged[0], offset, HEAD, 1)
        value_head = lax.dynamic_slice_in_dim(merged[1], offset, HEAD, 1)
        return dense_head(query_head, key_head, value_head)

    stacked = lax.map(one_head, head_ids)
    attention = jnp.transpose(stacked, (1, 0, 2)).reshape(rows_here, width).astype(jnp.bfloat16)
    blocks = lax.axis_size("fsdp")
    all_heads = lax.all_gather(attention, "fsdp", axis=1, tiled=True)
    columns = lax.all_to_all(out_weight, "fsdp", split_axis=1, concat_axis=0, tiled=True)
    heads_blocked = all_heads.reshape(rows_here, blocks, width)
    columns_blocked = columns.reshape(blocks, width, columns.shape[1])
    terms = jnp.einsum(
        "rfk,fkd->frd", heads_blocked, columns_blocked, preferred_element_type=jnp.float32
    )
    rounded = lax.optimization_barrier(terms.astype(jnp.bfloat16)).astype(jnp.float32)
    projected = jnp.sum(rounded, axis=0)
    gate_row = lax.dynamic_index_in_dim(gate_table, timestep[0], 0, keepdims=False)
    block_out = hidden_states[0].astype(jnp.float32) + gate_row[None, :] * projected
    return block_out.astype(jnp.bfloat16)[None]


MESH = pl.DeviceIdType.MESH
LEAD = 3


def attend_head(q_ref, q_cols, k_ref, v_ref, kv_cols, o_ref, o_cols):
    rows = q_ref.shape[0]
    tile = 128
    factor = HEAD ** (-0.5) * math.log2(math.e)
    keys = k_ref[:, kv_cols]
    values = v_ref[:, kv_cols]
    for start in range(0, rows, tile):
        part = slice(start, start + tile)
        scores = lax.dot_general(
            q_ref[part, q_cols], keys, (((1,), (1,)), ((), ())), preferred_element_type=jnp.float32
        )
        peak = jnp.max(scores, axis=-1, keepdims=True)
        weights = jnp.exp2((scores - peak) * factor)
        total = jnp.sum(weights, axis=-1, keepdims=True)
        summed = jnp.dot(weights.astype(jnp.bfloat16), values, preferred_element_type=jnp.float32)
        o_ref[part, o_cols] = (summed / total).astype(jnp.bfloat16)


def fused_kernel(
    far_heads, hidden_ref, q_hbm, fresh_ref, stale_ref, w_ref, gate_ref, out_ref,
    kv, q, helped_kv, helped_q, helped_out, att, att_peer, w_own, w_peer, hidden,
    local_sem, kv_send, kv_recv, edge_send, edge_recv, res_send, res_recv,
    att_send, att_recv, w_send, w_recv,
):
    rows, width = q.shape
    heads = width // HEAD
    last = lax.axis_size("patch") - 1
    near = heads - far_heads
    columns = w_own.shape[1]
    z = lax.axis_index("patch")
    f = lax.axis_index("fsdp")
    g = lax.axis_index("groups")
    c = lax.axis_index("cfg")
    is_edge = (z == 0) | (z == last)
    inner = jnp.logical_not(is_edge)
    inward = jnp.where(z == 0, 1, jnp.where(z == last, z - 1, z))
    edge = jnp.where(z <= 1, 0, last)
    edge_to = jnp.where(is_edge, jnp.where(z == 0, 1, last - 1), edge)

    def cols(t):
        return pl.ds(pl.multiple_of(t * HEAD, HEAD), HEAD)

    def span(p):
        return pl.ds(pl.multiple_of(p * rows, rows), rows)

    def remote(src, dst, send, recv, axis, index):
        return pltpu.make_async_remote_copy(
            src_ref=src, dst_ref=dst, send_sem=send, recv_sem=recv,
            device_id={axis: index}, device_id_type=MESH,
        )

    barrier = pltpu.get_barrier_semaphore()
    for axis in ("fsdp", "groups", "cfg"):
        pl.semaphore_signal(barrier, 1, device_id={axis: 1 - lax.axis_index(axis)}, device_id_type=MESH)

    @pl.when(z > 0)
    def _():
        pl.semaphore_signal(barrier, 1, device_id={"patch": z - 1}, device_id_type=MESH)

    @pl.when(z < last)
    def _():
        pl.semaphore_signal(barrier, 1, device_id={"patch": z + 1}, device_id_type=MESH)

    @pl.when(is_edge)
    def _():
        pl.semaphore_wait(barrier, 4)

    @pl.when(inner)
    def _():
        pl.semaphore_wait(barrier, 5)

    def kv_copy(way, hop, t):
        step = 1 if way == 0 else -1
        source = z - step * hop
        here = kv.at[:, span(source), cols(t)]
        src = stale_ref.at[0, :, :, cols(t)] if hop == 0 else here
        return remote(src, here, kv_send.at[way, hop, t], kv_recv.at[source, t], "patch", z + step)

    def kv_arrival(way, hop, t):
        step = 1 if way == 0 else -1
        source = z - step * hop
        here = kv.at[:, span(source), cols(t)]
        return remote(here, here, kv_send.at[way, 0, t], kv_recv.at[source, t], "patch", z - step)

    def source_there(way, hop):
        return z - hop >= 0 if way == 0 else z + hop <= last

    def may_send(way, t):
        if way == 0:
            return (z + 1 <= last) & ((z + 1 < last) | (t < near))
        return (z >= 1) & ((z - 1 > 0) | (t < near))

    def does_send(way, hop, t):
        return source_there(way, hop) & may_send(way, t)

    def does_receive(way, hop, t):
        return source_there(way, hop) & (inner | (t < near))

    def send_own(t):
        for way in (0, 1):
            @pl.when(does_send(way, 0, t))
            def _():
                kv_copy(way, 0, t).start()

    def take(hop, t):
        for way in (0, 1):
            @pl.when(does_receive(way, hop, t))
            def _():
                kv_arrival(way, hop, t).wait_recv()

            if hop < 3:
                @pl.when(does_send(way, hop, t))
                def _():
                    kv_copy(way, hop, t).start()

    def edge_q(i):
        return remote(
            q_hbm.at[0, :, cols(near + i)], helped_q.at[:, cols(i)],
            edge_send.at[0, i], edge_recv.at[0, i], "patch", edge_to)

    def edge_kv(i):
        return remote(
            fresh_ref.at[0, :, :, cols(near + i)],
            helped_kv.at[:, span(z), cols(i)],
            edge_send.at[1, i], edge_recv.at[1, i], "patch", edge_to)

    def edge_kv_arrival(i):
        here = helped_kv.at[:, span(edge), cols(i)]
        return remote(here, here, edge_send.at[1, i], edge_recv.at[1, i], "patch", edge_to)

    def result_copy(i):
        return remote(
            helped_out.at[:, cols(i)], att.at[:, cols(near + i)],
            res_send.at[i], res_recv.at[i], "patch", edge_to)

    def att_copy(t):
        return remote(att.at[:, cols(t)], att_peer.at[:, cols(t)], att_send.at[t], att_recv.at[t], "fsdp", 1 - f)

    quarter = w_peer.shape[0] // 4

    def w_rows(gi, ci):
        return pl.ds(pl.multiple_of((gi * 2 + ci) * quarter, quarter), quarter)

    def w_x():
        there = pl.ds(pl.multiple_of((1 - f) * columns, columns), columns)
        return remote(
            w_ref.at[w_rows(g, c), there], w_peer.at[w_rows(g, c), :],
            w_send.at[0], w_recv.at[0], "fsdp", 1 - f)

    def w_y():
        here = w_peer.at[w_rows(g, c), :]
        return remote(here, here, w_send.at[1], w_recv.at[1], "groups", 1 - g)

    def w_core(k):
        here = w_peer.at[w_rows(g if k == 0 else 1 - g, c), :]
        return remote(here, here, w_send.at[2 + k], w_recv.at[2 + k], "cfg", 1 - c)

    @pl.when(is_edge)
    def _():
        @pl.loop(0, heads)
        def _(t):
            send_own(t)

            @pl.when(t >= near)
            def _():
                edge_q(t - near).start()
                edge_kv(t - near).start()

    @pl.when(inner)
    def _():
        @pl.loop(0, LEAD)
        def _(t):
            send_own(t)

    w_x().start()
    q_in = pltpu.make_async_copy(q_hbm.at[0], q, local_sem.at[0])
    fresh_in = pltpu.make_async_copy(fresh_ref.at[0], kv.at[:, span(z), :], local_sem.at[1])
    hidden_in = pltpu.make_async_copy(hidden_ref.at[0], hidden, local_sem.at[2])
    w_in = pltpu.make_async_copy(
        w_ref.at[:, pl.ds(pl.multiple_of(f * columns, columns), columns)], w_own, local_sem.at[3])
    stale_in = pltpu.make_async_copy(
        stale_ref.at[0, :, :, pl.ds(near * HEAD, far_heads * HEAD)],
        helped_kv.at[:, span(z), :], local_sem.at[4])
    q_in.start()
    fresh_in.start()

    @pl.when(inner)
    def _():
        stale_in.start()

    hidden_in.start()
    w_in.start()
    q_in.wait()
    fresh_in.wait()

    @pl.when(inner)
    def _():
        stale_in.wait()

    take(1, 0)
    x_step = jnp.where(is_edge, 2, 4)
    y_step = jnp.where(is_edge, near, heads - 1)

    @pl.loop(0, heads)
    def _(t):
        @pl.when(inner & (t + LEAD < heads))
        def _():
            send_own(t + LEAD)

        @pl.when(t + 1 < heads)
        def _():
            take(1, t + 1)

        take(2, t)
        take(3, t)

        @pl.when(t == x_step)
        def _():
            w_x().wait_recv()
            w_y().start()
            w_core(0).start()

        @pl.when(t == y_step)
        def _():
            w_y().wait_recv()
            w_core(1).start()

        @pl.when(inner & (t >= near))
        def _():
            i = t - near
            edge_q(i).wait_recv()
            edge_kv_arrival(i).wait_recv()
            for p in range(4):
                @pl.when((z != p) & (edge != p))
                def _():
                    part = slice(p * rows, (p + 1) * rows)
                    helped_kv[:, part, cols(i)] = kv[:, part, cols(t)]
            attend_head(helped_q, cols(i), helped_kv.at[0], helped_kv.at[1], cols(i), helped_out, cols(i))
            result_copy(i).start()

        @pl.when(inner | (t < near))
        def _():
            attend_head(q, cols(t), kv.at[0], kv.at[1], cols(t), att, cols(t))

        @pl.when(is_edge & (t >= near))
        def _():
            result_copy(t - near).wait_recv()

        att_copy(t).start()

    w_in.wait()
    hidden_in.wait()
    w_core(0).wait_recv()
    w_core(1).wait_recv()

    @pl.loop(0, heads)
    def _(t):
        att_copy(t).wait_recv()

    step = 512

    @pl.loop(0, columns // step)
    def _(n):
        part = pl.ds(pl.multiple_of(n * step, step), step)
        mine = jnp.dot(att[...], w_own[:, part], preferred_element_type=jnp.float32)
        other = jnp.dot(att_peer[...], w_peer[:, part], preferred_element_type=jnp.float32)
        projected = mine.astype(jnp.bfloat16).astype(jnp.float32) + other.astype(jnp.bfloat16).astype(jnp.float32)
        moved = hidden[:, part].astype(jnp.float32) + gate_ref[:, part] * projected
        out_ref[:, part] = moved.astype(jnp.bfloat16)

    w_x().wait_send()
    w_y().wait_send()
    w_core(0).wait_send()
    w_core(1).wait_send()

    @pl.loop(0, heads)
    def _(t):
        att_copy(t).wait_send()
        for way in (0, 1):
            for hop in (0, 1, 2):
                @pl.when(does_send(way, hop, t))
                def _():
                    kv_copy(way, hop, t).wait_send()

    @pl.loop(0, far_heads)
    def _(i):
        @pl.when(is_edge)
        def _():
            edge_q(i).wait_send()
            edge_kv(i).wait_send()

        @pl.when(inner)
        def _():
            result_copy(i).wait_send()


def fused_local(hidden_states, queries, fresh_kv, stale_kv, out_weight, gate_table, timestep):
    rows, width = queries.shape[1:]
    heads = width // HEAD
    tokens = rows * lax.axis_size("patch")
    columns = hidden_states.shape[2]
    far_heads = (2 * heads) // 5
    gate_row = lax.dynamic_index_in_dim(gate_table, timestep[0], 0, keepdims=True)
    bf16 = jnp.bfloat16
    hbm = pl.BlockSpec(memory_space=pl.ANY)
    dma = pltpu.SemaphoreType.DMA
    out = pl.pallas_call(
        functools.partial(fused_kernel, far_heads),
        out_shape=jax.ShapeDtypeStruct((rows, columns), bf16),
        in_specs=[hbm] * 5 + [pl.BlockSpec(memory_space=pltpu.VMEM)],
        out_specs=pl.BlockSpec(memory_space=pltpu.VMEM),
        scratch_shapes=[
            pltpu.VMEM((2, tokens, width), bf16),
            pltpu.VMEM((rows, width), bf16),
            pltpu.VMEM((2, tokens, far_heads * HEAD), bf16),
            pltpu.VMEM((rows, far_heads * HEAD), bf16),
            pltpu.VMEM((rows, far_heads * HEAD), bf16),
            pltpu.VMEM((rows, width), bf16),
            pltpu.VMEM((rows, width), bf16),
            pltpu.VMEM((width, columns), bf16),
            pltpu.VMEM((width, columns), bf16),
            pltpu.VMEM((rows, columns), bf16),
            dma((5,)),
            dma((2, 3, heads)),
            dma((4, heads)),
            dma((2, far_heads)),
            dma((2, far_heads)),
            dma((far_heads,)),
            dma((far_heads,)),
            dma((heads,)),
            dma((heads,)),
            dma((4,)),
            dma((4,)),
        ],
        compiler_params=pltpu.CompilerParams(
            collective_id=0, has_side_effects=True, vmem_limit_bytes=56 << 20),
    )(hidden_states, queries, fresh_kv, stale_kv, out_weight, gate_row)
    return out[None]


def solution(mesh):
    in_specs = (
        P(("groups", "cfg"), "patch", "fsdp"),
        P(("groups", "cfg"), "patch", "fsdp"),
        P(("groups", "cfg"), None, "patch", "fsdp"),
        P(("groups", "cfg"), None, "patch", "fsdp"),
        P("fsdp", None),
        P(None, "fsdp"),
        P("groups"),
    )
    out_specs = P(("groups", "cfg"), "patch", "fsdp")
    body = local
    if mesh.shape["patch"] == 4 and mesh.shape["fsdp"] == 2 and mesh.shape["groups"] == 2 and mesh.shape["cfg"] == 2:
        body = fused_local
    return jax.shard_map(body, mesh=mesh, in_specs=in_specs, out_specs=out_specs, check_vma=False)
```

```python
import functools
import math

import jax
import jax.numpy as jnp
from jax import lax
from jax.experimental import pallas as pl
from jax.experimental.pallas import tpu as pltpu
from jax.sharding import PartitionSpec as P

HEAD = 128


def dense_head(query_head, key_head, value_head):
    scores = jnp.einsum(
        "qd,kd->qk", query_head, key_head, preferred_element_type=jnp.float32
    ) * HEAD ** (-0.5)
    peak = jnp.max(scores, axis=-1, keepdims=True)
    weights = jnp.exp(scores - peak)
    total = jnp.sum(weights, axis=-1, keepdims=True)
    probs = weights.astype(jnp.bfloat16)
    return jnp.dot(probs, value_head, preferred_element_type=jnp.float32) / total


def local(hidden_states, queries, fresh_kv, stale_kv, out_weight, gate_table, timestep):
    rows_here = queries.shape[1]
    width = queries.shape[2]
    heads_here = width // HEAD
    query_local = queries[0]
    own_start = lax.axis_index("patch") * rows_here
    head_ids = jnp.arange(heads_here, dtype=jnp.int32)
    gathered = lax.all_gather(stale_kv, "patch", axis=2, tiled=True)[0]
    merged = lax.dynamic_update_slice_in_dim(gathered, fresh_kv[0], own_start, 1)

    def one_head(head):
        offset = head * HEAD
        query_head = lax.dynamic_slice_in_dim(query_local, offset, HEAD, 1)
        key_head = lax.dynamic_slice_in_dim(merged[0], offset, HEAD, 1)
        value_head = lax.dynamic_slice_in_dim(merged[1], offset, HEAD, 1)
        return dense_head(query_head, key_head, value_head)

    stacked = lax.map(one_head, head_ids)
    attention = jnp.transpose(stacked, (1, 0, 2)).reshape(rows_here, width).astype(jnp.bfloat16)
    blocks = lax.axis_size("fsdp")
    all_heads = lax.all_gather(attention, "fsdp", axis=1, tiled=True)
    columns = lax.all_to_all(out_weight, "fsdp", split_axis=1, concat_axis=0, tiled=True)
    heads_blocked = all_heads.reshape(rows_here, blocks, width)
    columns_blocked = columns.reshape(blocks, width, columns.shape[1])
    terms = jnp.einsum(
        "rfk,fkd->frd", heads_blocked, columns_blocked, preferred_element_type=jnp.float32
    )
    rounded = lax.optimization_barrier(terms.astype(jnp.bfloat16)).astype(jnp.float32)
    projected = jnp.sum(rounded, axis=0)
    gate_row = lax.dynamic_index_in_dim(gate_table, timestep[0], 0, keepdims=False)
    block_out = hidden_states[0].astype(jnp.float32) + gate_row[None, :] * projected
    return block_out.astype(jnp.bfloat16)[None]


MESH = pl.DeviceIdType.MESH
LEAD = 3


def attend_head(q_ref, q_cols, k_ref, v_ref, kv_cols, o_ref, o_cols):
    rows = q_ref.shape[0]
    tile = 128
    factor = HEAD ** (-0.5) * math.log2(math.e)
    keys = k_ref[:, kv_cols]
    values = v_ref[:, kv_cols]
    for start in range(0, rows, tile):
        part = slice(start, start + tile)
        scores = lax.dot_general(
            q_ref[part, q_cols], keys, (((1,), (1,)), ((), ())), preferred_element_type=jnp.float32
        )
        peak = jnp.max(scores, axis=-1, keepdims=True)
        weights = jnp.exp2((scores - peak) * factor)
        total = jnp.sum(weights, axis=-1, keepdims=True)
        summed = jnp.dot(weights.astype(jnp.bfloat16), values, preferred_element_type=jnp.float32)
        o_ref[part, o_cols] = (summed / total).astype(jnp.bfloat16)


def fused_kernel(
    far_heads, hidden_ref, q_hbm, fresh_ref, stale_ref, w_ref, gate_ref, when_ref, out_ref,
    kv, q, helped_kv, helped_q, helped_out, att, att_peer, w_own, w_peer, hidden, gates, total,
    local_sem, kv_send, kv_recv, edge_send, edge_recv, res_send, res_recv,
    att_send, att_recv, w_send, w_recv,
):
    rows, width = q.shape
    heads = width // HEAD
    last = lax.axis_size("patch") - 1
    near = heads - far_heads
    columns = w_own.shape[1]
    z = lax.axis_index("patch")
    f = lax.axis_index("fsdp")
    g = lax.axis_index("groups")
    c = lax.axis_index("cfg")
    is_edge = (z == 0) | (z == last)
    inner = jnp.logical_not(is_edge)
    inward = jnp.where(z == 0, 1, jnp.where(z == last, z - 1, z))
    edge = jnp.where(z <= 1, 0, last)
    edge_to = jnp.where(is_edge, jnp.where(z == 0, 1, last - 1), edge)

    def cols(t):
        return pl.ds(pl.multiple_of(t * HEAD, HEAD), HEAD)

    def span(p):
        return pl.ds(pl.multiple_of(p * rows, rows), rows)

    def remote(src, dst, send, recv, axis, index):
        return pltpu.make_async_remote_copy(
            src_ref=src, dst_ref=dst, send_sem=send, recv_sem=recv,
            device_id={axis: index}, device_id_type=MESH,
        )

    barrier = pltpu.get_barrier_semaphore()
    for axis in ("fsdp", "groups", "cfg"):
        pl.semaphore_signal(barrier, 1, device_id={axis: 1 - lax.axis_index(axis)}, device_id_type=MESH)

    @pl.when(z > 0)
    def _():
        pl.semaphore_signal(barrier, 1, device_id={"patch": z - 1}, device_id_type=MESH)

    @pl.when(z < last)
    def _():
        pl.semaphore_signal(barrier, 1, device_id={"patch": z + 1}, device_id_type=MESH)

    @pl.when(is_edge)
    def _():
        pl.semaphore_wait(barrier, 4)

    @pl.when(inner)
    def _():
        pl.semaphore_wait(barrier, 5)

    def kv_copy(way, hop, t):
        step = 1 if way == 0 else -1
        source = z - step * hop
        here = kv.at[:, span(source), cols(t)]
        src = stale_ref.at[0, :, :, cols(t)] if hop == 0 else here
        return remote(src, here, kv_send.at[way, hop, t], kv_recv.at[source, t], "patch", z + step)

    def kv_arrival(way, hop, t):
        step = 1 if way == 0 else -1
        source = z - step * hop
        here = kv.at[:, span(source), cols(t)]
        return remote(here, here, kv_send.at[way, 0, t], kv_recv.at[source, t], "patch", z - step)

    def source_there(way, hop):
        return z - hop >= 0 if way == 0 else z + hop <= last

    def may_send(way, t):
        if way == 0:
            return (z + 1 <= last) & ((z + 1 < last) | (t < near))
        return (z >= 1) & ((z - 1 > 0) | (t < near))

    def does_send(way, hop, t):
        return source_there(way, hop) & may_send(way, t)

    def does_receive(way, hop, t):
        return source_there(way, hop) & (inner | (t < near))

    def send_own(t):
        for way in (0, 1):
            @pl.when(does_send(way, 0, t))
            def _():
                kv_copy(way, 0, t).start()

    def take(hop, t):
        for way in (0, 1):
            @pl.when(does_receive(way, hop, t))
            def _():
                kv_arrival(way, hop, t).wait_recv()

            if hop < 3:
                @pl.when(does_send(way, hop, t))
                def _():
                    kv_copy(way, hop, t).start()

    def edge_q(i):
        return remote(
            q_hbm.at[0, :, cols(near + i)], helped_q.at[:, cols(i)],
            edge_send.at[0, i], edge_recv.at[0, i], "patch", edge_to)

    def edge_kv(i):
        return remote(
            fresh_ref.at[0, :, :, cols(near + i)],
            helped_kv.at[:, span(z), cols(i)],
            edge_send.at[1, i], edge_recv.at[1, i], "patch", edge_to)

    def edge_kv_arrival(i):
        here = helped_kv.at[:, span(edge), cols(i)]
        return remote(here, here, edge_send.at[1, i], edge_recv.at[1, i], "patch", edge_to)

    def result_copy(i):
        return remote(
            helped_out.at[:, cols(i)], att.at[:, cols(near + i)],
            res_send.at[i], res_recv.at[i], "patch", edge_to)

    def att_copy(t):
        return remote(att.at[:, cols(t)], att_peer.at[:, cols(t)], att_send.at[t], att_recv.at[t], "fsdp", 1 - f)

    piece = w_peer.shape[0] // 16

    def w_rows(gi, ci, k):
        return pl.ds(pl.multiple_of(((gi * 2 + ci) * 4 + k) * piece, piece), piece)

    def w_x(k):
        there = pl.ds(pl.multiple_of((1 - f) * columns, columns), columns)
        return remote(
            w_ref.at[w_rows(g, c, k), there], w_peer.at[w_rows(g, c, k), :],
            w_send.at[0, k], w_recv.at[0, k], "fsdp", 1 - f)

    def w_y(k):
        here = w_peer.at[w_rows(g, c, k), :]
        return remote(here, here, w_send.at[1, k], w_recv.at[1, k], "groups", 1 - g)

    def w_core(hop, k):
        here = w_peer.at[w_rows(g if hop == 0 else 1 - g, c, k), :]
        return remote(here, here, w_send.at[2 + hop, k], w_recv.at[2 + hop, k], "cfg", 1 - c)

    @pl.when(is_edge)
    def _():
        @pl.loop(0, heads)
        def _(t):
            send_own(t)

            @pl.when(t >= near)
            def _():
                edge_q(t - near).start()
                edge_kv(t - near).start()

    @pl.when(inner)
    def _():
        @pl.loop(0, LEAD)
        def _(t):
            send_own(t)

    q_in = pltpu.make_async_copy(q_hbm.at[0], q, local_sem.at[0])
    fresh_in = pltpu.make_async_copy(fresh_ref.at[0], kv.at[:, span(z), :], local_sem.at[1])
    hidden_in = pltpu.make_async_copy(hidden_ref.at[0], hidden, local_sem.at[2])
    w_in = pltpu.make_async_copy(
        w_ref.at[:, pl.ds(pl.multiple_of(f * columns, columns), columns)], w_own, local_sem.at[3])
    stale_in = pltpu.make_async_copy(
        stale_ref.at[0, :, :, pl.ds(near * HEAD, far_heads * HEAD)],
        helped_kv.at[:, span(z), :], local_sem.at[4])
    q_in.start()
    fresh_in.start()

    @pl.when(inner)
    def _():
        stale_in.start()

    gates_in = pltpu.make_async_copy(gate_ref, gates, local_sem.at[5])
    hidden_in.start()
    gates_in.start()
    w_in.start()
    q_in.wait()
    fresh_in.wait()

    @pl.when(inner)
    def _():
        stale_in.wait()

    take(1, 0)
    early = heads - 2
    step = 512

    def project(begin, end, part):
        mine = jnp.dot(att[:, begin:end], w_own[begin:end, part], preferred_element_type=jnp.float32)
        return mine + jnp.dot(att_peer[:, begin:end], w_peer[begin:end, part], preferred_element_type=jnp.float32)

    @pl.loop(0, heads)
    def _(t):
        @pl.when(inner & (t + LEAD < heads))
        def _():
            send_own(t + LEAD)

        @pl.when(t + 1 < heads)
        def _():
            take(1, t + 1)

        @pl.when(t < 4)
        def _():
            w_x(t).start()

        @pl.when((t >= 2) & (t < 6))
        def _():
            w_x(t - 2).wait_recv()
            w_y(t - 2).start()
            w_core(0, t - 2).start()

        @pl.when((t >= 4) & (t < 8))
        def _():
            w_y(t - 4).wait_recv()
            w_core(1, t - 4).start()

        @pl.when(t == heads - 1)
        def _():
            for k in range(4):
                w_core(0, k).wait_recv()
                w_core(1, k).wait_recv()
            w_in.wait()

            @pl.loop(0, early)
            def _(h):
                att_copy(h).wait_recv()

            @pl.loop(0, columns // step)
            def _(n):
                part = pl.ds(pl.multiple_of(n * step, step), step)
                total[:, part] = project(0, early * HEAD, part)

        take(2, t)
        take(3, t)

        @pl.when(inner & (t >= near))
        def _():
            i = t - near
            edge_q(i).wait_recv()
            edge_kv_arrival(i).wait_recv()
            for p in range(4):
                @pl.when((z != p) & (edge != p))
                def _():
                    part = slice(p * rows, (p + 1) * rows)
                    helped_kv[:, part, cols(i)] = kv[:, part, cols(t)]
            attend_head(helped_q, cols(i), helped_kv.at[0], helped_kv.at[1], cols(i), helped_out, cols(i))
            result_copy(i).start()

        @pl.when(inner | (t < near))
        def _():
            attend_head(q, cols(t), kv.at[0], kv.at[1], cols(t), att, cols(t))

        @pl.when(is_edge & (t >= near))
        def _():
            result_copy(t - near).wait_recv()

        att_copy(t).start()

    hidden_in.wait()
    gates_in.wait()

    @pl.loop(early, heads)
    def _(t):
        att_copy(t).wait_recv()

    @pl.loop(0, columns // step)
    def _(n):
        part = pl.ds(pl.multiple_of(n * step, step), step)
        projected = total[:, part] + project(early * HEAD, heads * HEAD, part)
        gate = gates[pl.ds(when_ref[0], 1), part]
        moved = hidden[:, part].astype(jnp.float32) + gate * projected
        out_ref[:, part] = moved.astype(jnp.bfloat16)

    @pl.loop(0, 4)
    def _(k):
        w_x(k).wait_send()
        w_y(k).wait_send()
        w_core(0, k).wait_send()
        w_core(1, k).wait_send()

    @pl.loop(0, heads)
    def _(t):
        att_copy(t).wait_send()
        for way in (0, 1):
            for hop in (0, 1, 2):
                @pl.when(does_send(way, hop, t))
                def _():
                    kv_copy(way, hop, t).wait_send()

    @pl.loop(0, far_heads)
    def _(i):
        @pl.when(is_edge)
        def _():
            edge_q(i).wait_send()
            edge_kv(i).wait_send()

        @pl.when(inner)
        def _():
            result_copy(i).wait_send()


def fused_local(hidden_states, queries, fresh_kv, stale_kv, out_weight, gate_table, timestep):
    rows, width = queries.shape[1:]
    heads = width // HEAD
    tokens = rows * lax.axis_size("patch")
    columns = hidden_states.shape[2]
    far_heads = heads // 2
    bf16 = jnp.bfloat16
    hbm = pl.BlockSpec(memory_space=pl.ANY)
    dma = pltpu.SemaphoreType.DMA
    out = pl.pallas_call(
        functools.partial(fused_kernel, far_heads),
        out_shape=jax.ShapeDtypeStruct((rows, columns), bf16),
        in_specs=[hbm] * 6 + [pl.BlockSpec(memory_space=pltpu.SMEM)],
        out_specs=pl.BlockSpec(memory_space=pltpu.VMEM),
        scratch_shapes=[
            pltpu.VMEM((2, tokens, width), bf16),
            pltpu.VMEM((rows, width), bf16),
            pltpu.VMEM((2, tokens, far_heads * HEAD), bf16),
            pltpu.VMEM((rows, far_heads * HEAD), bf16),
            pltpu.VMEM((rows, far_heads * HEAD), bf16),
            pltpu.VMEM((rows, width), bf16),
            pltpu.VMEM((rows, width), bf16),
            pltpu.VMEM((width, columns), bf16),
            pltpu.VMEM((width, columns), bf16),
            pltpu.VMEM((rows, columns), bf16),
            pltpu.VMEM(gate_table.shape, jnp.float32),
            pltpu.VMEM((rows, columns), jnp.float32),
            dma((6,)),
            dma((2, 3, heads)),
            dma((4, heads)),
            dma((2, far_heads)),
            dma((2, far_heads)),
            dma((far_heads,)),
            dma((far_heads,)),
            dma((heads,)),
            dma((heads,)),
            dma((4, 4)),
            dma((4, 4)),
        ],
        compiler_params=pltpu.CompilerParams(
            collective_id=0, has_side_effects=True, vmem_limit_bytes=56 << 20),
    )(hidden_states, queries, fresh_kv, stale_kv, out_weight, gate_table, timestep)
    return out[None]


def solution(mesh):
    in_specs = (
        P(("groups", "cfg"), "patch", "fsdp"),
        P(("groups", "cfg"), "patch", "fsdp"),
        P(("groups", "cfg"), None, "patch", "fsdp"),
        P(("groups", "cfg"), None, "patch", "fsdp"),
        P("fsdp", None),
        P(None, "fsdp"),
        P("groups"),
    )
    out_specs = P(("groups", "cfg"), "patch", "fsdp")
    body = local
    if mesh.shape["patch"] == 4 and mesh.shape["fsdp"] == 2 and mesh.shape["groups"] == 2 and mesh.shape["cfg"] == 2:
        body = fused_local
    return jax.shard_map(body, mesh=mesh, in_specs=in_specs, out_specs=out_specs, check_vma=False)
```

```python
import functools
import math

import jax
import jax.numpy as jnp
from jax import lax
from jax.experimental import pallas as pl
from jax.experimental.pallas import tpu as pltpu
from jax.sharding import PartitionSpec as P

HEAD = 128


def dense_head(query_head, key_head, value_head):
    scores = jnp.einsum(
        "qd,kd->qk", query_head, key_head, preferred_element_type=jnp.float32
    ) * HEAD ** (-0.5)
    peak = jnp.max(scores, axis=-1, keepdims=True)
    weights = jnp.exp(scores - peak)
    total = jnp.sum(weights, axis=-1, keepdims=True)
    probs = weights.astype(jnp.bfloat16)
    return jnp.dot(probs, value_head, preferred_element_type=jnp.float32) / total


def local(hidden_states, queries, fresh_kv, stale_kv, out_weight, gate_table, timestep):
    rows_here = queries.shape[1]
    width = queries.shape[2]
    heads_here = width // HEAD
    query_local = queries[0]
    own_start = lax.axis_index("patch") * rows_here
    head_ids = jnp.arange(heads_here, dtype=jnp.int32)
    gathered = lax.all_gather(stale_kv, "patch", axis=2, tiled=True)[0]
    merged = lax.dynamic_update_slice_in_dim(gathered, fresh_kv[0], own_start, 1)

    def one_head(head):
        offset = head * HEAD
        query_head = lax.dynamic_slice_in_dim(query_local, offset, HEAD, 1)
        key_head = lax.dynamic_slice_in_dim(merged[0], offset, HEAD, 1)
        value_head = lax.dynamic_slice_in_dim(merged[1], offset, HEAD, 1)
        return dense_head(query_head, key_head, value_head)

    stacked = lax.map(one_head, head_ids)
    attention = jnp.transpose(stacked, (1, 0, 2)).reshape(rows_here, width).astype(jnp.bfloat16)
    blocks = lax.axis_size("fsdp")
    all_heads = lax.all_gather(attention, "fsdp", axis=1, tiled=True)
    columns = lax.all_to_all(out_weight, "fsdp", split_axis=1, concat_axis=0, tiled=True)
    heads_blocked = all_heads.reshape(rows_here, blocks, width)
    columns_blocked = columns.reshape(blocks, width, columns.shape[1])
    terms = jnp.einsum(
        "rfk,fkd->frd", heads_blocked, columns_blocked, preferred_element_type=jnp.float32
    )
    rounded = lax.optimization_barrier(terms.astype(jnp.bfloat16)).astype(jnp.float32)
    projected = jnp.sum(rounded, axis=0)
    gate_row = lax.dynamic_index_in_dim(gate_table, timestep[0], 0, keepdims=False)
    block_out = hidden_states[0].astype(jnp.float32) + gate_row[None, :] * projected
    return block_out.astype(jnp.bfloat16)[None]


MESH = pl.DeviceIdType.MESH
LEAD = 2
TILE = 128
AHEAD = 2


def attend_head(q_ref, q_cols, k_ref, v_ref, kv_cols, o_ref, o_cols, done):
    rows = q_ref.shape[0]
    factor = HEAD ** (-0.5) * math.log2(math.e)
    keys = k_ref[:, kv_cols]
    values = v_ref[:, kv_cols]
    for r in range(rows // TILE):
        part = slice(r * TILE, (r + 1) * TILE)
        scores = lax.dot_general(
            q_ref[part, q_cols], keys, (((1,), (1,)), ((), ())), preferred_element_type=jnp.float32
        )
        peak = jnp.max(scores, axis=-1, keepdims=True)
        weights = jnp.exp2((scores - peak) * factor)
        total = jnp.sum(weights, axis=-1, keepdims=True)
        summed = jnp.dot(weights.astype(jnp.bfloat16), values, preferred_element_type=jnp.float32)
        o_ref[part, o_cols] = (summed / total).astype(jnp.bfloat16)
        done(r)


def fused_kernel(
    far_heads, hidden_ref, q_hbm, fresh_ref, stale_ref, w_ref, gate_ref, when_ref, out_ref,
    kv, q, helped_kv, helped_q, helped_out, att, att_peer, w_own, w_peer, hidden, gates, total,
    local_sem, kv_send, kv_recv, edge_send, edge_recv, res_send, res_recv,
    att_send, att_recv, w_send, w_recv,
):
    rows, width = q.shape
    heads = width // HEAD
    last = lax.axis_size("patch") - 1
    near = heads - far_heads
    columns = w_own.shape[1]
    z = lax.axis_index("patch")
    f = lax.axis_index("fsdp")
    g = lax.axis_index("groups")
    c = lax.axis_index("cfg")
    is_edge = (z == 0) | (z == last)
    inner = jnp.logical_not(is_edge)
    inward = jnp.where(z == 0, 1, jnp.where(z == last, z - 1, z))
    edge = jnp.where(z <= 1, 0, last)
    edge_to = jnp.where(is_edge, jnp.where(z == 0, 1, last - 1), edge)

    def cols(t):
        return pl.ds(pl.multiple_of(t * HEAD, HEAD), HEAD)

    def span(p):
        return pl.ds(pl.multiple_of(p * rows, rows), rows)

    def remote(src, dst, send, recv, axis, index):
        return pltpu.make_async_remote_copy(
            src_ref=src, dst_ref=dst, send_sem=send, recv_sem=recv,
            device_id={axis: index}, device_id_type=MESH,
        )

    barrier = pltpu.get_barrier_semaphore()
    for axis in ("fsdp", "groups", "cfg"):
        pl.semaphore_signal(barrier, 1, device_id={axis: 1 - lax.axis_index(axis)}, device_id_type=MESH)

    @pl.when(z > 0)
    def _():
        pl.semaphore_signal(barrier, 1, device_id={"patch": z - 1}, device_id_type=MESH)

    @pl.when(z < last)
    def _():
        pl.semaphore_signal(barrier, 1, device_id={"patch": z + 1}, device_id_type=MESH)

    @pl.when(is_edge)
    def _():
        pl.semaphore_wait(barrier, 4)

    @pl.when(inner)
    def _():
        pl.semaphore_wait(barrier, 5)

    def kv_copy(way, hop, t):
        step = 1 if way == 0 else -1
        source = z - step * hop
        here = kv.at[:, span(source), cols(t)]
        src = stale_ref.at[0, :, :, cols(t)] if hop == 0 else here
        return remote(src, here, kv_send.at[way, hop, t], kv_recv.at[source, t], "patch", z + step)

    def kv_arrival(way, hop, t):
        step = 1 if way == 0 else -1
        source = z - step * hop
        here = kv.at[:, span(source), cols(t)]
        return remote(here, here, kv_send.at[way, 0, t], kv_recv.at[source, t], "patch", z - step)

    def source_there(way, hop):
        return z - hop >= 0 if way == 0 else z + hop <= last

    def may_send(way, t):
        if way == 0:
            return (z + 1 <= last) & ((z + 1 < last) | (t < near))
        return (z >= 1) & ((z - 1 > 0) | (t < near))

    def does_send(way, hop, t):
        return source_there(way, hop) & may_send(way, t)

    def does_receive(way, hop, t):
        return source_there(way, hop) & (inner | (t < near))

    def send_own(t):
        for way in (0, 1):
            @pl.when(does_send(way, 0, t))
            def _():
                kv_copy(way, 0, t).start()

    def take(hop, t):
        for way in (0, 1):
            @pl.when(does_receive(way, hop, t))
            def _():
                kv_arrival(way, hop, t).wait_recv()

            if hop < 3:
                @pl.when(does_send(way, hop, t))
                def _():
                    kv_copy(way, hop, t).start()

    def edge_q(i):
        return remote(
            q_hbm.at[0, :, cols(near + i)], helped_q.at[:, cols(i)],
            edge_send.at[0, i], edge_recv.at[0, i], "patch", edge_to)

    def edge_kv(i):
        return remote(
            fresh_ref.at[0, :, :, cols(near + i)],
            helped_kv.at[:, span(z), cols(i)],
            edge_send.at[1, i], edge_recv.at[1, i], "patch", edge_to)

    def edge_kv_arrival(i):
        here = helped_kv.at[:, span(edge), cols(i)]
        return remote(here, here, edge_send.at[1, i], edge_recv.at[1, i], "patch", edge_to)

    tiles = rows // TILE

    def result_copy(i, r):
        part = slice(r * TILE, (r + 1) * TILE)
        return remote(
            helped_out.at[part, cols(i)], att.at[part, cols(near + i)],
            res_send.at[i, r], res_recv.at[i, r], "patch", edge_to)

    def att_copy(t, r):
        part = slice(r * TILE, (r + 1) * TILE)
        return remote(
            att.at[part, cols(t)], att_peer.at[part, cols(t)],
            att_send.at[t, r], att_recv.at[t, r], "fsdp", 1 - f)

    piece = w_peer.shape[0] // 16

    def w_rows(gi, ci, k):
        return pl.ds(pl.multiple_of((k * 4 + gi * 2 + ci) * piece, piece), piece)

    def w_x(k):
        there = pl.ds(pl.multiple_of((1 - f) * columns, columns), columns)
        return remote(
            w_ref.at[w_rows(g, c, k), there], w_peer.at[w_rows(g, c, k), :],
            w_send.at[0, k], w_recv.at[0, k], "fsdp", 1 - f)

    def w_y(k):
        here = w_peer.at[w_rows(g, c, k), :]
        return remote(here, here, w_send.at[1, k], w_recv.at[1, k], "groups", 1 - g)

    def w_core(hop, k):
        here = w_peer.at[w_rows(g if hop == 0 else 1 - g, c, k), :]
        return remote(here, here, w_send.at[2 + hop, k], w_recv.at[2 + hop, k], "cfg", 1 - c)

    @pl.when(inner)
    def _():
        @pl.loop(0, LEAD)
        def _(t):
            send_own(t)

    q_in = pltpu.make_async_copy(q_hbm.at[0], q, local_sem.at[0])
    fresh_in = pltpu.make_async_copy(fresh_ref.at[0], kv.at[:, span(z), :], local_sem.at[1])
    hidden_in = pltpu.make_async_copy(hidden_ref.at[0], hidden, local_sem.at[2])
    w_in = pltpu.make_async_copy(
        w_ref.at[:, pl.ds(pl.multiple_of(f * columns, columns), columns)], w_own, local_sem.at[3])
    stale_in = pltpu.make_async_copy(
        stale_ref.at[0, :, :, pl.ds(near * HEAD, far_heads * HEAD)],
        helped_kv.at[:, span(z), :], local_sem.at[4])
    q_in.start()
    fresh_in.start()

    @pl.when(inner)
    def _():
        stale_in.start()

    gates_in = pltpu.make_async_copy(gate_ref, gates, local_sem.at[5])
    hidden_in.start()
    gates_in.start()
    w_in.start()
    q_in.wait()
    fresh_in.wait()

    @pl.when(inner)
    def _():
        stale_in.wait()

    def w_tick(u):
        @pl.when(u < 4)
        def _():
            w_x(u).start()

        @pl.when((u >= 2) & (u < 6))
        def _():
            w_x(u - 2).wait_recv()
            w_y(u - 2).start()
            w_core(0, u - 2).start()

        @pl.when((u >= 4) & (u < 8))
        def _():
            w_y(u - 4).wait_recv()
            w_core(1, u - 4).start()

    @pl.when(is_edge)
    def _():
        @pl.loop(0, heads)
        def _(m):
            send_own(m)

            @pl.when(m % 2 == 0)
            def _():
                w_tick(m // 2)

            for way in (0, 1):
                @pl.when((m >= AHEAD) & does_send(way, 0, m))
                def _():
                    kv_copy(way, 0, m - AHEAD).wait_send()

    take(1, 0)
    early = heads - 2
    half = early // 2
    step = 512

    def w_taken(k):
        w_core(0, k).wait_recv()
        w_core(1, k).wait_recv()

    def att_taken(begin, end):
        @pl.loop(begin, end)
        def _(h):
            for r in range(tiles):
                att_copy(h, r).wait_recv()

    def add_up(left, right, begin, end, first):
        deep = slice(begin * HEAD, end * HEAD)

        @pl.loop(0, columns // step)
        def _(n):
            part = pl.ds(pl.multiple_of(n * step, step), step)
            term = jnp.dot(left[:, deep], right[deep, part], preferred_element_type=jnp.float32)
            total[:, part] = term if first else total[:, part] + term

    @pl.loop(0, heads)
    def _(t):
        @pl.when(inner & (t + LEAD < heads))
        def _():
            send_own(t + LEAD)

        @pl.when(t + 1 < heads)
        def _():
            take(1, t + 1)

        w_tick(jnp.where(is_edge, t + heads // 2, t))

        @pl.when(is_edge & (t < far_heads))
        def _():
            edge_q(t).start()
            edge_kv(t).start()

        take(2, t)
        take(3, t)

        @pl.when(inner & (t >= near))
        def _():
            i = t - near
            edge_q(i).wait_recv()
            edge_kv_arrival(i).wait_recv()
            for p in range(4):
                @pl.when((z != p) & (edge != p))
                def _():
                    part = slice(p * rows, (p + 1) * rows)
                    helped_kv[:, part, cols(i)] = kv[:, part, cols(t)]
            attend_head(helped_q, cols(i), helped_kv.at[0], helped_kv.at[1], cols(i), helped_out, cols(i),
                        lambda r: result_copy(i, r).start())

        @pl.when(t == half)
        def _():
            w_in.wait()
            add_up(att, w_own, 0, half, True)

        @pl.when(t == heads - 4)
        def _():
            w_taken(0)
            w_taken(1)
            att_taken(0, half)
            add_up(att_peer, w_peer, 0, half, False)

        @pl.when(t == heads - 2)
        def _():
            add_up(att, w_own, half, early, False)

        @pl.when(t == heads - 1)
        def _():
            w_taken(2)
            w_taken(3)
            att_taken(half, early)
            add_up(att_peer, w_peer, half, early, False)

        @pl.when(inner | (t < near))
        def _():
            attend_head(q, cols(t), kv.at[0], kv.at[1], cols(t), att, cols(t),
                        lambda r: att_copy(t, r).start())

        @pl.when(is_edge & (t >= near))
        def _():
            for r in range(tiles):
                result_copy(t - near, r).wait_recv()
                att_copy(t, r).start()

    hidden_in.wait()
    gates_in.wait()
    add_up(att, w_own, early, heads, False)

    att_taken(early, heads)

    @pl.loop(0, columns // step)
    def _(n):
        part = pl.ds(pl.multiple_of(n * step, step), step)
        projected = total[:, part] + jnp.dot(
            att_peer[:, early * HEAD:], w_peer[early * HEAD:, part], preferred_element_type=jnp.float32)
        gate = gates[pl.ds(when_ref[0], 1), part]
        moved = hidden[:, part].astype(jnp.float32) + gate * projected
        out_ref[:, part] = moved.astype(jnp.bfloat16)

    @pl.loop(0, 4)
    def _(k):
        w_x(k).wait_send()
        w_y(k).wait_send()
        w_core(0, k).wait_send()
        w_core(1, k).wait_send()

    @pl.loop(0, heads)
    def _(t):
        for r in range(tiles):
            att_copy(t, r).wait_send()
        for way in (0, 1):
            for hop in (0, 1, 2):
                waited = is_edge & (t < heads - AHEAD) if hop == 0 else False
                @pl.when(does_send(way, hop, t) & jnp.logical_not(waited))
                def _():
                    kv_copy(way, hop, t).wait_send()

    @pl.loop(0, far_heads)
    def _(i):
        @pl.when(is_edge)
        def _():
            edge_q(i).wait_send()
            edge_kv(i).wait_send()

        @pl.when(inner)
        def _():
            for r in range(tiles):
                result_copy(i, r).wait_send()


def fused_local(hidden_states, queries, fresh_kv, stale_kv, out_weight, gate_table, timestep):
    rows, width = queries.shape[1:]
    heads = width // HEAD
    tokens = rows * lax.axis_size("patch")
    columns = hidden_states.shape[2]
    far_heads = heads // 2
    bf16 = jnp.bfloat16
    hbm = pl.BlockSpec(memory_space=pl.ANY)
    dma = pltpu.SemaphoreType.DMA
    out = pl.pallas_call(
        functools.partial(fused_kernel, far_heads),
        out_shape=jax.ShapeDtypeStruct((rows, columns), bf16),
        in_specs=[hbm] * 6 + [pl.BlockSpec(memory_space=pltpu.SMEM)],
        out_specs=pl.BlockSpec(memory_space=pltpu.VMEM),
        scratch_shapes=[
            pltpu.VMEM((2, tokens, width), bf16),
            pltpu.VMEM((rows, width), bf16),
            pltpu.VMEM((2, tokens, far_heads * HEAD), bf16),
            pltpu.VMEM((rows, far_heads * HEAD), bf16),
            pltpu.VMEM((rows, far_heads * HEAD), bf16),
            pltpu.VMEM((rows, width), bf16),
            pltpu.VMEM((rows, width), bf16),
            pltpu.VMEM((width, columns), bf16),
            pltpu.VMEM((width, columns), bf16),
            pltpu.VMEM((rows, columns), bf16),
            pltpu.VMEM(gate_table.shape, jnp.float32),
            pltpu.VMEM((rows, columns), jnp.float32),
            dma((6,)),
            dma((2, 3, heads)),
            dma((4, heads)),
            dma((2, far_heads)),
            dma((2, far_heads)),
            dma((far_heads, rows // TILE)),
            dma((far_heads, rows // TILE)),
            dma((heads, rows // TILE)),
            dma((heads, rows // TILE)),
            dma((4, 4)),
            dma((4, 4)),
        ],
        compiler_params=pltpu.CompilerParams(
            collective_id=0, has_side_effects=True, vmem_limit_bytes=56 << 20),
    )(hidden_states, queries, fresh_kv, stale_kv, out_weight, gate_table, timestep)
    return out[None]


def solution(mesh):
    in_specs = (
        P(("groups", "cfg"), "patch", "fsdp"),
        P(("groups", "cfg"), "patch", "fsdp"),
        P(("groups", "cfg"), None, "patch", "fsdp"),
        P(("groups", "cfg"), None, "patch", "fsdp"),
        P("fsdp", None),
        P(None, "fsdp"),
        P("groups"),
    )
    out_specs = P(("groups", "cfg"), "patch", "fsdp")
    body = local
    if mesh.shape["patch"] == 4 and mesh.shape["fsdp"] == 2 and mesh.shape["groups"] == 2 and mesh.shape["cfg"] == 2:
        body = fused_local
    return jax.shard_map(body, mesh=mesh, in_specs=in_specs, out_specs=out_specs, check_vma=False)
```
